256 devices in a mesh: wide: 16 (over z, core), narrow: 16 (over x, y).
Axes of the slice: x: 4, y: 4, z: 8, core: 2. Of those that a mesh axis runs over, the one named last changes fastest.
Arguments:
- amplitudes: float32 [4, 64, 640, 640], P(None, 'wide', None, 'narrow'), may hold values from -6 to 6
- cycle_block: float32 [64, 640, 4, 640], P('wide', 'narrow'), may hold values from -0.078125 to 0.078125
- occupied_irreps: int32 [64], replicated, may hold values from 0 to 7, as said below
- virtual_irreps: int32 [640], replicated, may hold values from 0 to 7, as said below
- slab_orbitals: int32 [4], replicated, may hold values from 0 to 63, as said below
Outputs:
- cycle_residual: float32 [4, 4, 640, 640], P(None, None, 'narrow', 'wide')
The draws below stay inside these ranges and needn't reach their ends.
Inputs may be any that keep to these rules, and one draw needn't show every extreme that they name: `occupied_irreps`: nondecreasing; every irrep 0 to 7 labels at least 4 orbitals. `virtual_irreps`: nondecreasing; every irrep 0 to 7 labels at least 64 orbitals. `slab_orbitals`: distinct occupied orbital indices in increasing order; the last is 63.
All inputs are finite; a program needn't handle non-finite values.
Results may differ from the reference program's by a relative error of at most 0.0003.
Values sent between devices are 32-bit elements; how exact they have to be, the bound alone decides.
No kernel may reach another device: no remote copies, remote signals or barrier semaphores. Data moves between devices by JAX's collectives and lax.ppermute only.
A program may use at most 128 MiB of HBM per device.

```python
import jax
import jax.numpy as jnp
from jax import lax

O = 64
V = 640
NI = 4
OBLK = 4
VBLK = 64


def draw_labels(key, count, least):
    base = jnp.repeat(jnp.arange(8, dtype=jnp.int32), least)
    extra = jax.random.randint(key, (count - 8 * least,), 0, 8, dtype=jnp.int32)
    return jnp.sort(jnp.concatenate([base, extra])).astype(jnp.int32)


def draw_occupied_irreps(key, part):
    return draw_labels(jax.random.fold_in(key, 11), O, OBLK)


def draw_virtual_irreps(key, part):
    return draw_labels(jax.random.fold_in(key, 12), V, VBLK)


def draw_slab_orbitals(key, part):
    order = jax.random.permutation(jax.random.fold_in(key, 13), O - 1).astype(jnp.int32)
    chosen = jnp.sort(order[:NI - 1]).astype(jnp.int32)
    last = jnp.full((1,), O - 1, dtype=jnp.int32)
    return jnp.concatenate([chosen, last]).astype(jnp.int32)


def levels(own_key, shape, cuts, low, high):
    def one(position, blocks):
        steps = jax.random.uniform(jax.random.fold_in(jax.random.fold_in(own_key, 6), position), (blocks,), jnp.float32, low / len(cuts), high / len(cuts))
        return jnp.repeat(jnp.exp(steps), shape[position] // blocks).reshape((-1,) + (1,) * (len(shape) - position - 1))

    loudness = one(*cuts[0])
    for cut in cuts[1:]:
        loudness = loudness * one(*cut)
    return loudness


def noise(own_key, shape, scale, bound, shards=(), kind=jnp.bfloat16):
    result = scale * jax.random.normal(own_key, shape, jnp.float32)
    if shards:
        result = result * levels(own_key, shape, shards, -0.22, 0.18)
    return jnp.clip(result, -bound, bound).astype(kind)


def setup_inputs(seed: int = 0) -> dict:
    splits = jax.random.split(jax.random.key(seed), 6)
    return {
        "amplitudes": noise(splits[0], (NI, O, V, V), 1.0, 6.0, ((1, 16), (3, 16)), jnp.float32),
        "cycle_block": noise(splits[1], (O, V, NI, V), (O * V // 8) ** -0.5, 0.078125, ((0, 16), (1, 16)), jnp.float32),
        "occupied_irreps": draw_occupied_irreps(jax.random.fold_in(splits[5], 71), 0),
        "virtual_irreps": draw_virtual_irreps(jax.random.fold_in(splits[5], 71), 0),
        "slab_orbitals": draw_slab_orbitals(jax.random.fold_in(splits[5], 71), 0),
    }


def select_sym(values, first, second, third, fourth):
    labels = jnp.bitwise_xor(jnp.bitwise_xor(first[:, None, None, None], second[None, :, None, None]), jnp.bitwise_xor(third[None, None, :, None], fourth[None, None, None, :]))
    return jnp.where(labels == 0, values, jnp.zeros_like(values))


def reference(amplitudes, cycle_block, occupied_irreps, virtual_irreps, slab_orbitals):
    orbits = jnp.arange(occupied_irreps.shape[0], dtype=jnp.int32)
    slab_irreps = jnp.sum(jnp.where(orbits[None, :] == slab_orbitals[:, None], occupied_irreps[None, :], 0), axis=1).astype(jnp.int32)
    kept_cycle = select_sym(cycle_block, occupied_irreps, virtual_irreps, slab_irreps, virtual_irreps)

    def single(pair):
        row, label = pair
        kept = select_sym(row[None], label[None], occupied_irreps, virtual_irreps, virtual_irreps)[0]
        return jnp.einsum("kac,kcjb->jab", kept, kept_cycle, precision=lax.Precision.HIGHEST)

    return lax.map(single, (amplitudes, slab_irreps))
```

```python
import functools

import jax
import jax.numpy as jnp
import numpy as np
from jax import lax
from jax.experimental import pallas as pl
from jax.experimental.pallas import tpu as pltpu
from jax.sharding import PartitionSpec as P

SMEM = pl.BlockSpec(memory_space=pltpu.SMEM)
VMEM = pl.BlockSpec(memory_space=pltpu.VMEM)
LIMIT = 48 * 1024 * 1024
CLASSES = 8
NARROW_F = 64
WIDE_F = 128
FAST_Q = 6
SLAB, FLAG, PLACE = 8, 12, 16


def params():
    return pltpu.CompilerParams(vmem_limit_bytes=LIMIT)


def iota(shape, dim):
    return lax.broadcasted_iota(jnp.int32, shape, dim)


def class_of(table, index):
    label = jnp.zeros_like(index)
    for x in range(1, CLASSES):
        label = label + (index >= table[x]).astype(jnp.int32)
    return label


def table_kernel(occ, vir, slab, table):
    v = vir[...].astype(jnp.float32)
    table[0] = 0
    starts = [jnp.int32(0)]
    for x in range(1, CLASSES):
        start = jnp.sum((v < x).astype(jnp.float32)).astype(jnp.int32)
        table[x] = start
        starts.append(start)
    starts.append(jnp.int32(vir.shape[0] * vir.shape[1]))

    def before(t, half):
        rest = lax.rem(t, 80) - 40 * half
        return lax.div(t, 80) * 40 + jnp.minimum(jnp.maximum(rest, 0), 40)

    widest = jnp.int32(0)
    for x in range(CLASSES):
        for half in range(2):
            widest = jnp.maximum(widest, before(starts[x + 1], half) - before(starts[x], half))
    s = [occ[slab[i]] for i in range(4)]
    for i in range(4):
        table[SLAB + i] = s[i]
    labels = [s[i] ^ s[j] for i in range(4) for j in range(4)]
    most = jnp.int32(0)
    for p in range(16):
        place = jnp.int32(0)
        for r in range(p):
            place = place + (labels[r] == labels[p]).astype(jnp.int32)
        table[PLACE + p] = place
        most = jnp.maximum(most, place)
    table[FLAG] = jnp.logical_and(widest <= NARROW_F, most < FAST_Q).astype(jnp.int32)
    for t in (13, 14, 15):
        table[t] = 0


def make_table(occ, vir, slab):
    return pl.pallas_call(
        table_kernel,
        out_shape=jax.ShapeDtypeStruct((32,), jnp.int32),
        in_specs=[SMEM, VMEM, SMEM],
        out_specs=SMEM,
        name="table",
    )(occ, vir.reshape(5, 128), slab)


def row_labels(table, occ, wide, narrow):
    row = iota((160, 1), 0)
    k = (row >= 40).astype(jnp.int32) + (row >= 80).astype(jnp.int32) + (row >= 120).astype(jnp.int32)
    label = jnp.zeros_like(row)
    for q in range(4):
        label = jnp.where(k == q, occ[wide * 4 + q], label)
    return label ^ class_of(table, row - 40 * k + 40 * narrow)


def halves(x):
    hi = x.astype(jnp.bfloat16)
    return hi, (x - hi.astype(jnp.float32)).astype(jnp.bfloat16)


def fold_matrix(f):
    b = np.arange(640)
    out = np.zeros((640, 2 * f), np.float32)
    out[b, (b // 40 % 2) * f + (b // 80 * 40 + b % 40) % f] = 1
    return jnp.asarray(out, jnp.bfloat16)


def fold_kernel(f, table, occ, w, pick, own, other):
    wide, narrow = lax.axis_index("wide"), lax.axis_index("narrow")
    rows = row_labels(table, occ, wide, narrow)
    cols = class_of(table, iota((1, 640), 1))
    even = lax.rem(wide, 2) == 0
    parts = []
    for j in range(4):
        keep = (rows ^ table[SLAB + j]) == cols
        hi, lo = halves(jnp.where(keep, w[:, j, :], 0.0))
        parts.append(
            jnp.dot(hi, pick[...], preferred_element_type=jnp.float32)
            + jnp.dot(lo, pick[...], preferred_element_type=jnp.float32)
        )
    if f == 128:
        for j in range(4):
            zero, one = parts[j][:, :128], parts[j][:, 128:]
            own[:, j * 128:(j + 1) * 128] = jnp.where(even, zero, one)
            other[:, j * 128:(j + 1) * 128] = jnp.where(even, one, zero)
    else:
        low = iota((160, 128), 1) < 64
        for p in range(2):
            x, y = parts[2 * p], parts[2 * p + 1]
            zero = jnp.where(low, x, pltpu.roll(y, 64, 1))
            one = jnp.where(low, pltpu.roll(x, 64, 1), y)
            own[:, p * 128:(p + 1) * 128] = jnp.where(even, zero, one)
            other[:, p * 128:(p + 1) * 128] = jnp.where(even, one, zero)


def fold(f, table, occ, w):
    shape = jax.ShapeDtypeStruct((160, 4 * f), jnp.float32)
    own, other = pl.pallas_call(
        functools.partial(fold_kernel, f),
        out_shape=(shape, shape),
        in_specs=[SMEM, SMEM, VMEM, VMEM],
        out_specs=(VMEM, VMEM),
        compiler_params=params(),
        name="fold",
    )(table, occ, w, fold_matrix(f))
    return own, swap(other)


def swap(x):
    return lax.ppermute(x, "wide", [(d, d ^ 1) for d in range(16)])


def product_kernel(f, table, occ, a_own, a_other, w_own, w_other, out):
    i = pl.program_id(0)
    wide, narrow = lax.axis_index("wide"), lax.axis_index("narrow")
    cols = class_of(table, iota((1, 640), 1)) ^ table[SLAB + i]
    his, los = [], []
    for a, at in ((a_own, wide), (a_other, wide ^ 1)):
        keep = row_labels(table, occ, at, narrow) == cols
        hi, lo = halves(jnp.where(keep, a[0], 0.0))
        his.append(hi)
        los.append(lo)
    w0, v0 = halves(w_own[...])
    w1, v1 = halves(w_other[...])
    left = jnp.concatenate(his + los + his, axis=0)
    right = jnp.concatenate([w0, w1, w0, w1, v0, v1], axis=0)
    r = lax.dot_general(left, right, (((0,), (0,)), ((), ())), preferred_element_type=jnp.float32)
    out[...] = r.reshape(16, 40, 4 * f)


def product(f, table, occ, a_own, a_other, w_own, w_other):
    block = pl.BlockSpec((1, 160, 640), lambda i: (i, 0, 0))
    whole = pl.BlockSpec((160, 4 * f), lambda i: (0, 0))
    return pl.pallas_call(
        functools.partial(product_kernel, f),
        out_shape=jax.ShapeDtypeStruct((16, 160, 4 * f), jnp.float32),
        grid=(4,),
        in_specs=[SMEM, SMEM, block, block, whole, whole],
        out_specs=pl.BlockSpec((16, 40, 4 * f), lambda i: (0, i, 0)),
        compiler_params=params(),
        name="product",
    )(table, occ, a_own, a_other, w_own, w_other)


def spread_kernel(f, q, table, got, out, acc):
    wide, narrow = lax.axis_index("wide"), lax.axis_index("narrow")
    acls = class_of(table, iota((40, 1), 0) + 40 * narrow)
    u = iota((1, 384), 1)
    block = jnp.zeros_like(u)
    for t in range(1, 8):
        block = block + (u >= 40 * t).astype(jnp.int32)
    plane = acls ^ class_of(table, u + 40 * block + 40 * lax.rem(wide, 2))
    acc[...] = jnp.zeros_like(acc)
    low = iota((40, 128), 1) < 64
    for i in range(4):
        r = got[0, i * 40:(i + 1) * 40, :]
        for n in range(1, 16):
            r = r + got[n, i * 40:(i + 1) * 40, :]
        for j in range(4):
            if f == 128:
                value = r[:, j * 128:(j + 1) * 128]
            else:
                x = r[:, j // 2 * 128:(j // 2 + 1) * 128]
                y = pltpu.roll(x, 64, 1)
                value = jnp.where(low, x, y) if j % 2 == 0 else jnp.where(low, y, x)
            keep = plane == (table[SLAB + i] ^ table[SLAB + j])
            at = table[PLACE + 4 * i + j]
            acc[at] += jnp.where(keep, jnp.concatenate([value] * 3, axis=1), 0.0)
    pad = out.shape[2] - 40 * q
    for z in range(8):
        pieces = [acc[p, :, 40 * z:40 * z + 40] for p in range(q)]
        if pad:
            pieces.append(jnp.zeros((40, pad), jnp.float32))
        out[z] = jnp.concatenate(pieces, axis=1)


def spread(f, q, table, got):
    lanes = -(-40 * q // 128) * 128
    return pl.pallas_call(
        functools.partial(spread_kernel, f, q),
        out_shape=jax.ShapeDtypeStruct((8, 40, lanes), jnp.float32),
        in_specs=[SMEM, VMEM],
        out_specs=VMEM,
        scratch_shapes=[pltpu.VMEM((q, 40, 384), jnp.float32)],
        compiler_params=params(),
        name="spread",
    )(table, got)


def finish_kernel(q, table, got, out, acc):
    wide, narrow = lax.axis_index("wide"), lax.axis_index("narrow")
    acls = class_of(table, iota((40, 1), 0) + 40 * narrow)
    plane = acls ^ class_of(table, iota((1, 40), 1) + 40 * wide)
    r = got[0]
    for z in range(1, 8):
        r = r + got[z]
    for p in range(q):
        acc[p] = r[:, 40 * p:40 * p + 40]
    for i in range(4):
        for j in range(4):
            keep = plane == (table[SLAB + i] ^ table[SLAB + j])
            out[i, j] = jnp.where(keep, acc[table[PLACE + 4 * i + j]], 0.0)


def finish(q, table, got):
    return pl.pallas_call(
        functools.partial(finish_kernel, q),
        out_shape=jax.ShapeDtypeStruct((4, 4, 40, 40), jnp.float32),
        in_specs=[SMEM, VMEM],
        out_specs=VMEM,
        scratch_shapes=[pltpu.VMEM((q, 40, 40), jnp.float32)],
        compiler_params=params(),
        name="finish",
    )(table, got)


def rest(f, q, table, occ, a_own, a_other, w_own, w_other):
    sent = product(f, table, occ, a_own, a_other, w_own, w_other)
    got = lax.all_to_all(sent, "narrow", 0, 0)
    slots = spread(f, q, table, got)
    same_core = [[c + 2 * z for z in range(8)] for c in range(2)]
    return finish(q, table, lax.all_to_all(slots, "wide", 0, 0, axis_index_groups=same_core))


def local(amplitudes, cycle_block, occ, vir, slab):
    a_own = jnp.transpose(amplitudes, (0, 1, 3, 2)).reshape(4, 160, 640)
    a_other = swap(a_own)
    w = cycle_block.reshape(160, 4, 640)
    table = make_table(occ, vir, slab)
    w_own, w_other = fold(NARROW_F, table, occ, w)

    def fast(w, w_own, w_other):
        return rest(NARROW_F, FAST_Q, table, occ, a_own, a_other, w_own, w_other)

    def general(w, w_own, w_other):
        own, other = fold(WIDE_F, table, occ, w)
        return rest(WIDE_F, 16, table, occ, a_own, a_other, own, other)

    return lax.cond(table[FLAG] == 1, fast, general, w, w_own, w_other)


def solution(mesh):
    placed = (P(None, "wide", None, "narrow"), P("wide", "narrow", None, None), P(), P(), P())
    return jax.shard_map(
        local,
        mesh=mesh,
        in_specs=placed,
        out_specs=P(None, None, "narrow", "wide"),
        check_vma=False,
    )
```

```python
import functools

import jax
import jax.numpy as jnp
import numpy as np
from jax import lax
from jax.experimental import pallas as pl
from jax.experimental.pallas import tpu as pltpu
from jax.sharding import PartitionSpec as P

SMEM = pl.BlockSpec(memory_space=pltpu.SMEM)
VMEM = pl.BlockSpec(memory_space=pltpu.VMEM)
LIMIT = 48 * 1024 * 1024
CLASSES = 8
PACKED, ANY = 192, 512
SHORT, ALL = 6, 16
SLAB, FORM, PLACE, COUNT, SHIFT = 8, 12, 16, 32, 64


def params():
    return pltpu.CompilerParams(vmem_limit_bytes=LIMIT)


def iota(shape, dim):
    return lax.broadcasted_iota(jnp.int32, shape, dim)


def class_of(table, index):
    label = jnp.zeros_like(index)
    for x in range(1, CLASSES):
        label = label + (index >= table[x]).astype(jnp.int32)
    return label


def table_kernel(occ, vir, slab, table):
    v = vir[...].astype(jnp.float32)
    table[0] = 0
    starts = [jnp.int32(0)]
    for x in range(1, CLASSES):
        start = jnp.sum((v < x).astype(jnp.float32)).astype(jnp.int32)
        table[x] = start
        starts.append(start)
    starts.append(jnp.int32(vir.shape[0] * vir.shape[1]))

    def before(t, half):
        rest = lax.rem(t, 80) - 40 * half
        return lax.div(t, 80) * 40 + jnp.minimum(jnp.maximum(rest, 0), 40)

    marks = [[before(t, half) for t in starts] for half in range(2)]
    for half in range(2):
        for x in range(CLASSES):
            table[COUNT + 8 * half + x] = marks[half][x + 1] - marks[half][x]
    s = [occ[slab[i]] for i in range(4)]
    for i in range(4):
        table[SLAB + i] = s[i]
    labels = [s[i] ^ s[j] for i in range(4) for j in range(4)]
    most = jnp.int32(0)
    for p in range(16):
        place = jnp.int32(0)
        for r in range(p):
            place = place + (labels[r] == labels[p]).astype(jnp.int32)
        table[PLACE + p] = place
        most = jnp.maximum(most, place)
    widest = jnp.int32(0)
    for half in range(2):
        for j in range(4):
            for x in range(CLASSES):
                offset = jnp.int32(0)
                for other in range(j):
                    offset = offset + table[COUNT + 8 * half + (x ^ s[j] ^ s[other])]
                table[SHIFT + 32 * half + 8 * j + x] = offset - marks[half][x]
                if j == 3:
                    widest = jnp.maximum(widest, offset + table[COUNT + 8 * half + x])
    packed = (widest <= PACKED).astype(jnp.int32)
    table[FORM] = packed * (1 + (most < SHORT).astype(jnp.int32))


def make_table(occ, vir, slab):
    return pl.pallas_call(
        table_kernel,
        out_shape=jax.ShapeDtypeStruct((128,), jnp.int32),
        in_specs=[SMEM, VMEM, SMEM],
        out_specs=SMEM,
        name="table",
    )(occ, vir.reshape(5, 128), slab)


def row_labels(table, occ, wide, narrow):
    row = iota((160, 1), 0)
    k = (row >= 40).astype(jnp.int32) + (row >= 80).astype(jnp.int32) + (row >= 120).astype(jnp.int32)
    label = jnp.zeros_like(row)
    for q in range(4):
        label = jnp.where(k == q, occ[wide * 4 + q], label)
    return label ^ class_of(table, row - 40 * k + 40 * narrow)


def halves(x):
    hi = x.astype(jnp.bfloat16)
    return hi, (x - hi.astype(jnp.float32)).astype(jnp.bfloat16)


def fold_kernel(lanes, table, occ, w, own, other):
    wide, narrow = lax.axis_index("wide"), lax.axis_index("narrow")
    rows = row_labels(table, occ, wide, narrow)
    b = iota((1, 640), 1)
    cols = class_of(table, b)
    block = jnp.zeros_like(b)
    for t in range(1, 16):
        block = block + (b >= 40 * t).astype(jnp.int32)
    half = block & 1
    u = b - 40 * (block - (block >> 1))
    column = iota((lanes, 640), 0)
    mine = lax.rem(wide, 2)
    sums = [None, None]
    for j in range(4):
        keep = (rows ^ table[SLAB + j]) == cols
        hi, lo = halves(jnp.where(keep, w[:, j, :], 0.0))
        for side, at in enumerate((mine, 1 - mine)):
            shift = jnp.zeros_like(b)
            for x in range(CLASSES):
                shift = jnp.where(cols == x, table[SHIFT + 32 * at + 8 * j + x], shift)
            pick = (column == jnp.where(half == at, u + shift, -1)).astype(jnp.float32).astype(jnp.bfloat16)
            for part in (hi, lo):
                term = lax.dot_general(part, pick, (((1,), (1,)), ((), ())), preferred_element_type=jnp.float32)
                sums[side] = term if sums[side] is None else sums[side] + term
    own[...] = sums[0]
    other[...] = sums[1]


def fold(lanes, table, occ, w):
    shape = jax.ShapeDtypeStruct((160, lanes), jnp.float32)
    own, other = pl.pallas_call(
        functools.partial(fold_kernel, lanes),
        out_shape=(shape, shape),
        in_specs=[SMEM, SMEM, VMEM],
        out_specs=(VMEM, VMEM),
        compiler_params=params(),
        name="fold",
    )(table, occ, w)
    return own, swap(other)


def swap(x):
    return lax.ppermute(x, "wide", [(d, d ^ 1) for d in range(16)])


def product_kernel(lanes, table, occ, a_own, a_other, w_own, w_other, out):
    wide, narrow = lax.axis_index("wide"), lax.axis_index("narrow")
    w0, v0 = halves(w_own[...])
    w1, v1 = halves(w_other[...])
    right = jnp.concatenate([w0, w1, w0, w1, v0, v1], axis=0)
    rows = [row_labels(table, occ, at, narrow) for at in (wide, wide ^ 1)]
    both = []
    for step in range(2):
        cols = class_of(table, iota((1, 640), 1)) ^ table[SLAB + 2 * pl.program_id(0) + step]
        his, los = [], []
        for a, row in zip((a_own, a_other), rows):
            hi, lo = halves(jnp.where(row == cols, a[step], 0.0))
            his.append(hi)
            los.append(lo)
        left = jnp.concatenate(his + los + his, axis=0)
        r = lax.dot_general(left, right, (((0,), (0,)), ((), ())), preferred_element_type=jnp.float32)
        if lanes == 256:
            out[:, 40 * step:40 * step + 40, :] = r[:, :128].reshape(16, 40, 128)
            both.append(r[:, 128:])
        else:
            out[:, 40 * step:40 * step + 40, :] = r.reshape(16, 40, lanes)
    if both:
        tails = jnp.where(iota((640, 128), 1) < 64, both[0], pltpu.roll(both[1], 64, 1))
        out[:, 80:, :] = tails.reshape(16, 40, 128)


def product(lanes, table, occ, a_own, a_other, w_own, w_other):
    block = pl.BlockSpec((2, 160, 640), lambda p: (p, 0, 0))
    whole = pl.BlockSpec((160, lanes), lambda p: (0, 0))
    rows, wide = (120, 128) if lanes == 256 else (80, lanes)
    return pl.pallas_call(
        functools.partial(product_kernel, lanes),
        out_shape=jax.ShapeDtypeStruct((16, 2 * rows, wide), jnp.float32),
        grid=(2,),
        in_specs=[SMEM, SMEM, block, block, whole, whole],
        out_specs=pl.BlockSpec((16, rows, wide), lambda p: (0, p, 0)),
        compiler_params=params(),
        name="product",
    )(table, occ, a_own, a_other, w_own, w_other)


def spread_kernel(lanes, q, table, got, out, acc):
    wide, narrow = lax.axis_index("wide"), lax.axis_index("narrow")
    core = lax.rem(wide, 2)
    acls = class_of(table, iota((40, 1), 0) + 40 * narrow)
    u = iota((1, 384), 1)
    block = jnp.zeros_like(u)
    for t in range(1, 8):
        block = block + (u >= 40 * t).astype(jnp.int32)
    bcls = class_of(table, u + 40 * block + 40 * core)
    first, last = jnp.int32(0), jnp.int32(0)
    for x in range(1, CLASSES):
        first = first + (40 * narrow >= table[x]).astype(jnp.int32)
        last = last + (40 * narrow + 39 >= table[x]).astype(jnp.int32)
    acc[...] = jnp.zeros_like(acc)
    span = 80 if lanes == 512 else 120
    for p in range(2):
        r = got[0, p * span:(p + 1) * span, :]
        for n in range(1, 16):
            r = r + got[n, p * span:(p + 1) * span, :]
        for step in range(2):
            i = 2 * p + step
            value = r[40 * step:40 * step + 40]
            if lanes == 256:
                tail = r[80:] if step == 0 else pltpu.roll(r[80:], 64, 1)
                value = jnp.concatenate([value, tail, tail], axis=1)
            size = value.shape[1]
            for j in range(4):
                pair = table[SLAB + i] ^ table[SLAB + j]
                at = table[PLACE + 4 * i + j]
                x, y = first ^ pair, last ^ pair
                shift = table[SHIFT + 32 * core + 8 * j + x]
                one = pltpu.roll(value, lax.rem(size - shift, size), 1)[:, :384]
                shift = table[SHIFT + 32 * core + 8 * j + y]
                two = pltpu.roll(value, lax.rem(size - shift, size), 1)[:, :384]
                found = jnp.where(acls == first, one, two)
                acc[at] += jnp.where((acls ^ bcls) == pair, found, 0.0)
    pad = out.shape[2] - 40 * q
    for z in range(8):
        pieces = [acc[p, :, 40 * z:40 * z + 40] for p in range(q)]
        if pad:
            pieces.append(jnp.zeros((40, pad), jnp.float32))
        out[z] = jnp.concatenate(pieces, axis=1)


def spread(lanes, q, table, got):
    wide = -(-40 * q // 128) * 128
    return pl.pallas_call(
        functools.partial(spread_kernel, lanes, q),
        out_shape=jax.ShapeDtypeStruct((8, 40, wide), jnp.float32),
        in_specs=[SMEM, VMEM],
        out_specs=VMEM,
        scratch_shapes=[pltpu.VMEM((q, 40, 384), jnp.float32)],
        compiler_params=params(),
        name="spread",
    )(table, got)


def finish_kernel(q, table, got, out, acc):
    wide, narrow = lax.axis_index("wide"), lax.axis_index("narrow")
    acls = class_of(table, iota((40, 1), 0) + 40 * narrow)
    plane = acls ^ class_of(table, iota((1, 40), 1) + 40 * wide)
    r = got[0]
    for z in range(1, 8):
        r = r + got[z]
    for p in range(q):
        acc[p] = r[:, 40 * p:40 * p + 40]
    for i in range(4):
        for j in range(4):
            keep = plane == (table[SLAB + i] ^ table[SLAB + j])
            out[i, j] = jnp.where(keep, acc[table[PLACE + 4 * i + j]], 0.0)


def finish(q, table, got):
    return pl.pallas_call(
        functools.partial(finish_kernel, q),
        out_shape=jax.ShapeDtypeStruct((4, 4, 40, 40), jnp.float32),
        in_specs=[SMEM, VMEM],
        out_specs=VMEM,
        scratch_shapes=[pltpu.VMEM((q, 40, 40), jnp.float32)],
        compiler_params=params(),
        name="finish",
    )(table, got)


def rest(lanes, q, table, occ, a_own, a_other, w_own, w_other):
    sent = product(lanes, table, occ, a_own, a_other, w_own, w_other)
    got = lax.all_to_all(sent, "narrow", 0, 0)
    slots = spread(lanes, q, table, got)
    same_core = [[c + 2 * z for z in range(8)] for c in range(2)]
    return finish(q, table, lax.all_to_all(slots, "wide", 0, 0, axis_index_groups=same_core))


def local(amplitudes, cycle_block, occ, vir, slab):
    a_own = jnp.transpose(amplitudes, (0, 1, 3, 2)).reshape(4, 160, 640)
    a_other = swap(a_own)
    w = cycle_block.reshape(160, 4, 640)
    table = make_table(occ, vir, slab)
    w_own, w_other = fold(256, table, occ, w)

    def general(w, w_own, w_other):
        own, other = fold(ANY, table, occ, w)
        return rest(ANY, ALL, table, occ, a_own, a_other, own, other)

    def packed(w, w_own, w_other):
        return rest(256, ALL, table, occ, a_own, a_other, w_own, w_other)

    def short(w, w_own, w_other):
        return rest(256, SHORT, table, occ, a_own, a_other, w_own, w_other)

    return lax.switch(table[FORM], [general, packed, short], w, w_own, w_other)


def solution(mesh):
    placed = (P(None, "wide", None, "narrow"), P("wide", "narrow", None, None), P(), P(), P())
    return jax.shard_map(
        local,
        mesh=mesh,
        in_specs=placed,
        out_specs=P(None, None, "narrow", "wide"),
        check_vma=False,
    )
```

```python
import functools

import jax
import jax.numpy as jnp
import numpy as np
from jax import lax
from jax.experimental import pallas as pl
from jax.experimental.pallas import tpu as pltpu
from jax.sharding import PartitionSpec as P

SMEM = pl.BlockSpec(memory_space=pltpu.SMEM)
VMEM = pl.BlockSpec(memory_space=pltpu.VMEM)
LIMIT = 48 * 1024 * 1024
CLASSES = 8
TIGHT, PACKED, ANY = 170, 192, 512
LEAST, SHORT, ALL = 4, 6, 16
SLAB, PLACE, COUNT, SHIFT = 8, 16, 32, 64


def params():
    return pltpu.CompilerParams(vmem_limit_bytes=LIMIT)


def iota(shape, dim):
    return lax.broadcasted_iota(jnp.int32, shape, dim)


def class_of(table, index):
    label = jnp.zeros_like(index)
    for x in range(1, CLASSES):
        label = label + (index >= table[x]).astype(jnp.int32)
    return label


def fill_table(occ, vir, slab, table, form):
    v = vir[...].astype(jnp.float32)
    table[0] = 0
    starts = [jnp.int32(0)]
    for x in range(1, CLASSES):
        start = jnp.sum((v < x).astype(jnp.float32)).astype(jnp.int32)
        table[x] = start
        starts.append(start)
    starts.append(jnp.int32(vir.shape[0] * vir.shape[1]))

    def before(t, half):
        rest = lax.rem(t, 80) - 40 * half
        return lax.div(t, 80) * 40 + jnp.minimum(jnp.maximum(rest, 0), 40)

    marks = [[before(t, half) for t in starts] for half in range(2)]
    for half in range(2):
        for x in range(CLASSES):
            table[COUNT + 8 * half + x] = marks[half][x + 1] - marks[half][x]
    s = [occ[slab[i]] for i in range(4)]
    for i in range(4):
        table[SLAB + i] = s[i]
    labels = [s[i] ^ s[j] for i in range(4) for j in range(4)]
    most = jnp.int32(0)
    for p in range(16):
        place = jnp.int32(0)
        for r in range(p):
            place = place + (labels[r] == labels[p]).astype(jnp.int32)
        table[PLACE + p] = place
        most = jnp.maximum(most, place)
    widest = jnp.int32(0)
    for half in range(2):
        for j in range(4):
            for x in range(CLASSES):
                offset = jnp.int32(0)
                for other in range(j):
                    offset = offset + table[COUNT + 8 * half + (x ^ s[j] ^ s[other])]
                table[SHIFT + 32 * half + 8 * j + x] = offset - marks[half][x]
                if j == 3:
                    widest = jnp.maximum(widest, offset + table[COUNT + 8 * half + x])
    packed = (widest <= PACKED).astype(jnp.int32)
    form[0] = packed * (1 + (most < SHORT).astype(jnp.int32))


def row_labels(table, occ, wide, narrow):
    row = iota((160, 1), 0)
    k = (row >= 40).astype(jnp.int32) + (row >= 80).astype(jnp.int32) + (row >= 120).astype(jnp.int32)
    label = jnp.zeros_like(row)
    for q in range(4):
        label = jnp.where(k == q, occ[wide * 4 + q], label)
    return label ^ class_of(table, row - 40 * k + 40 * narrow)


def halves(x):
    hi = x.astype(jnp.bfloat16)
    return hi, (x - hi.astype(jnp.float32)).astype(jnp.bfloat16)


def fold_halves(lanes, table, occ, w, own, other):
    wide, narrow = lax.axis_index("wide"), lax.axis_index("narrow")
    rows = row_labels(table, occ, wide, narrow)
    b = iota((1, 640), 1)
    cols = class_of(table, b)
    block = jnp.zeros_like(b)
    for t in range(1, 16):
        block = block + (b >= 40 * t).astype(jnp.int32)
    half = block & 1
    u = b - 40 * (block - (block >> 1))
    column = iota((lanes, 640), 0)
    mine = lax.rem(wide, 2)
    left, picks = [], [[], []]
    for j in range(4):
        keep = (rows ^ table[SLAB + j]) == cols
        left.append(jnp.concatenate(halves(jnp.where(keep, w[:, j, :], 0.0)), axis=0))
        for side, at in enumerate((mine, 1 - mine)):
            shift = jnp.zeros_like(b)
            for x in range(CLASSES):
                shift = jnp.where(cols == x, table[SHIFT + 32 * at + 8 * j + x], shift)
            place = jnp.where(half == at, u + shift, -1)
            picks[side].append((column == place).astype(jnp.float32).astype(jnp.bfloat16))
    left = jnp.concatenate(left, axis=1)
    for side, out in enumerate((own, other)):
        pick = jnp.concatenate(picks[side], axis=1)
        r = lax.dot_general(left, pick, (((1,), (1,)), ((), ())), preferred_element_type=jnp.float32)
        out[:, :lanes] = r[:160] + r[160:]
        if lanes < out.shape[1]:
            out[:, lanes:] = jnp.zeros((160, out.shape[1] - lanes), jnp.float32)


def first_kernel(occ, vir, slab, w, table, form, own, other, held, sem):
    copy = pltpu.make_async_copy(w, held, sem)
    copy.start()
    fill_table(occ, vir, slab, table, form)
    copy.wait()
    fold_halves(PACKED, table, occ, held, own, other)


def first(occ, vir, slab, w):
    shape = jax.ShapeDtypeStruct((160, 256), jnp.float32)
    return pl.pallas_call(
        first_kernel,
        out_shape=(jax.ShapeDtypeStruct((128,), jnp.int32), jax.ShapeDtypeStruct((1,), jnp.int32), shape, shape),
        in_specs=[SMEM, VMEM, SMEM, pl.BlockSpec(memory_space=pltpu.HBM)],
        out_specs=(SMEM, SMEM, VMEM, VMEM),
        scratch_shapes=[pltpu.VMEM((160, 4, 640), jnp.float32), pltpu.SemaphoreType.DMA],
        compiler_params=params(),
        name="first",
    )(occ, vir.reshape(5, 128), slab, w)


def fold_any(table, occ, w):
    shape = jax.ShapeDtypeStruct((160, ANY), jnp.float32)
    return pl.pallas_call(
        functools.partial(fold_halves, ANY),
        out_shape=(shape, shape),
        in_specs=[SMEM, SMEM, VMEM],
        out_specs=(VMEM, VMEM),
        compiler_params=params(),
        name="fold",
    )(table, occ, w)


def swap(x):
    return lax.ppermute(x, "wide", [(d, d ^ 1) for d in range(16)])


def beside(parts, step):
    lane = iota(parts[0].shape, 1)
    out = parts[0]
    for t in range(1, len(parts)):
        out = jnp.where(lane < step * t, out, pltpu.roll(parts[t], step * t, 1))
    return out


def product_kernel(form, table, occ, a_own, a_other, w_own, w_other, out):
    wide, narrow = lax.axis_index("wide"), lax.axis_index("narrow")
    w0, v0 = halves(w_own[...])
    w1, v1 = halves(w_other[...])
    right = jnp.concatenate([w0, w1, w0, w1, v0, v1], axis=0)
    rows = [row_labels(table, occ, at, narrow) for at in (wide, wide ^ 1)]
    tails = []
    for i in range(4):
        cols = class_of(table, iota((1, 640), 1)) ^ table[SLAB + i]
        his, los = [], []
        for a, row in zip((a_own, a_other), rows):
            hi, lo = halves(jnp.where(row == cols, a[i], 0.0))
            his.append(hi)
            los.append(lo)
        left = jnp.concatenate(his + los + his, axis=0)
        r = lax.dot_general(left, right, (((0,), (0,)), ((), ())), preferred_element_type=jnp.float32)
        width = out.shape[2]
        out[:, 40 * i:40 * i + 40, :] = r[:, :width].reshape(16, 40, width)
        tails.append(r[:, 128:256])
    if form == PACKED:
        out[:, 160:200, :] = beside(tails[:2], 64).reshape(16, 40, 128)
        out[:, 200:240, :] = beside(tails[2:], 64).reshape(16, 40, 128)
    elif form == TIGHT:
        out[:, 160:200, :] = beside(tails[:3], 42).reshape(16, 40, 128)
        lane = iota((16, 16, 128), 2)
        last = [pltpu.roll(tails[3], 42 * t, 1) if t else tails[3] for t in range(3)]
        last = [x.reshape(16, 40, 128)[:, at:at + 16] for x, at in zip(last, (0, 16, 24))]
        out[:, 200:216, :] = jnp.where(lane < 42, last[0], jnp.where(lane < 84, last[1], last[2]))


def product(form, table, occ, a_own, a_other, w_own, w_other):
    shape = {TIGHT: (16, 216, 128), PACKED: (16, 240, 128), ANY: (16, 160, 512)}[form]
    return pl.pallas_call(
        functools.partial(product_kernel, form),
        out_shape=jax.ShapeDtypeStruct(shape, jnp.float32),
        in_specs=[SMEM, SMEM, VMEM, VMEM, VMEM, VMEM],
        out_specs=VMEM,
        compiler_params=params(),
        name="product",
    )(table, occ, a_own, a_other, w_own, w_other)


def tail_of(form, r, i):
    if form == PACKED:
        rows = r[160 + 40 * (i // 2):200 + 40 * (i // 2)]
        return pltpu.roll(rows, 64, 1) if i % 2 else rows
    if i < 3:
        return pltpu.roll(r[160:200], 128 - 42 * i, 1) if i else r[160:200]
    rows = r[200:216]
    return jnp.concatenate([rows, pltpu.roll(rows, 86, 1), pltpu.roll(rows, 44, 1)[8:16]], axis=0)


def spread_kernel(form, q, table, got, out, acc):
    wide, narrow = lax.axis_index("wide"), lax.axis_index("narrow")
    core = lax.rem(wide, 2)
    acls = class_of(table, iota((40, 1), 0) + 40 * narrow)
    u = iota((1, 384), 1)
    block = jnp.zeros_like(u)
    for t in range(1, 8):
        block = block + (u >= 40 * t).astype(jnp.int32)
    bcls = class_of(table, u + 40 * block + 40 * core)
    first, last = jnp.int32(0), jnp.int32(0)
    for x in range(1, CLASSES):
        first = first + (40 * narrow >= table[x]).astype(jnp.int32)
        last = last + (40 * narrow + 39 >= table[x]).astype(jnp.int32)
    acc[...] = jnp.zeros_like(acc)
    r = got[0]
    for n in range(1, 16):
        r = r + got[n]
    for i in range(4):
        value = r[40 * i:40 * i + 40]
        if form != ANY:
            tail = tail_of(form, r, i)
            value = jnp.concatenate([value, tail, tail], axis=1)
        size = value.shape[1]
        for j in range(4):
            pair = table[SLAB + i] ^ table[SLAB + j]
            at = table[PLACE + 4 * i + j]
            x, y = first ^ pair, last ^ pair
            shift = table[SHIFT + 32 * core + 8 * j + x]
            one = pltpu.roll(value, lax.rem(size - shift, size), 1)[:, :384]
            shift = table[SHIFT + 32 * core + 8 * j + y]
            two = pltpu.roll(value, lax.rem(size - shift, size), 1)[:, :384]
            found = jnp.where(acls == first, one, two)
            acc[at] += jnp.where((acls ^ bcls) == pair, found, 0.0)
    pad = -40 * q % 128
    for z in range(8):
        pieces = [acc[p, :, 40 * z:40 * z + 40] for p in range(q)]
        if pad:
            pieces.append(jnp.zeros((40, pad), jnp.float32))
        slot = jnp.concatenate(pieces, axis=1)
        if q == LEAST:
            out[z, :40] = slot[:, :128]
            groups = [slot[0:16, 128:160], slot[16:32, 128:160], slot[24:40, 128:160], slot[0:16, 160:192]]
            out[z, 40:] = jnp.concatenate(groups, axis=1)
        else:
            out[z] = slot


def slot_shape(q):
    return (8, 56, 128) if q == LEAST else (8, 40, -(-40 * q // 128) * 128)


def spread(form, q, table, got):
    return pl.pallas_call(
        functools.partial(spread_kernel, form, q),
        out_shape=jax.ShapeDtypeStruct(slot_shape(q), jnp.float32),
        in_specs=[SMEM, VMEM],
        out_specs=VMEM,
        scratch_shapes=[pltpu.VMEM((q, 40, 384), jnp.float32)],
        compiler_params=params(),
        name="spread",
    )(table, got)


def finish_kernel(q, table, got, out, acc):
    wide, narrow = lax.axis_index("wide"), lax.axis_index("narrow")
    acls = class_of(table, iota((40, 1), 0) + 40 * narrow)
    plane = acls ^ class_of(table, iota((1, 40), 1) + 40 * wide)
    r = got[0]
    for z in range(1, 8):
        r = r + got[z]
    if q == LEAST:
        tail = jnp.concatenate([r[40:, 0:32], r[40:, 32:64], r[48:, 64:96]], axis=0)
        r = jnp.concatenate([r[:40], tail], axis=1)
    for p in range(q):
        acc[p] = r[:, 40 * p:40 * p + 40]
    for i in range(4):
        for j in range(4):
            keep = plane == (table[SLAB + i] ^ table[SLAB + j])
            out[i, j] = jnp.where(keep, acc[table[PLACE + 4 * i + j]], 0.0)


def finish(q, table, got):
    shape = (4, 4, 40, 40)
    return pl.pallas_call(
        functools.partial(finish_kernel, q),
        out_shape=jax.ShapeDtypeStruct(shape, jnp.float32),
        in_specs=[SMEM, VMEM],
        out_specs=VMEM,
        scratch_shapes=[pltpu.VMEM((q, 40, 40), jnp.float32)],
        compiler_params=params(),
        name="finish",
    )(table, got)


def rest(form, q, table, occ, a_own, a_other, w_own, w_other):
    sent = product(form, table, occ, a_own, a_other, w_own, w_other)
    got = lax.all_to_all(sent, "narrow", 0, 0)
    slots = spread(form, q, table, got)
    same_core = [[c + 2 * z for z in range(8)] for c in range(2)]
    return finish(q, table, lax.all_to_all(slots, "wide", 0, 0, axis_index_groups=same_core))


def local(amplitudes, cycle_block, occ, vir, slab):
    a_own = jnp.transpose(amplitudes, (0, 1, 3, 2)).reshape(4, 160, 640)
    a_other = swap(a_own)
    w = cycle_block.reshape(160, 4, 640)
    table, form, w_own, w_other = first(occ, vir, slab, w)
    w_other = swap(w_other)

    def general(w, w_own, w_other):
        own, other = fold_any(table, occ, w)
        return rest(ANY, ALL, table, occ, a_own, a_other, own, swap(other))

    def packed(form, q):
        return lambda w, w_own, w_other: rest(form, q, table, occ, a_own, a_other, w_own, w_other)

    forms = [general, packed(PACKED, ALL), packed(PACKED, SHORT)]
    return lax.switch(form.reshape(()), forms, w, w_own, w_other)


def solution(mesh):
    placed = (P(None, "wide", None, "narrow"), P("wide", "narrow", None, None), P(), P(), P())
    return jax.shard_map(
        local,
        mesh=mesh,
        in_specs=placed,
        out_specs=P(None, None, "narrow", "wide"),
        check_vma=False,
    )
```
